128 devices in a mesh: seq: 32 (over x, y, core), kvh: 4 (over z).
Axes of the slice: x: 4, y: 4, z: 4, core: 2. Of those that a mesh axis runs over, the one named last changes fastest.
Arguments:
- queries: bfloat16 [16384, 8192], P(('seq', 'kvh')), may hold values from -8 to 8
- new_kv: bfloat16 [2, 16384, 1024], P(None, 'seq', 'kvh'), may hold values from -8 to 8
- cache_kv: bfloat16 [2, 262144, 1024], P(None, 'seq', 'kvh'), may hold values from -6 to 6
- vertical_blocks: int32 [8, 32], P('kvh'), may hold values from 0 to 4087, as said below
- slash_offsets: int32 [64, 3], P('kvh'), may hold values from 0 to 7, as said below
Outputs:
- attended: bfloat16 [16384, 8192], P(('seq', 'kvh'))
The draws below stay inside these ranges and needn't reach their ends.
Inputs may be any that keep to these rules, and one draw needn't show every extreme that they name: `vertical_blocks`: entries of a row are distinct cache block indices; none lies in the last 512 tokens of the cache. At most 4 entries of a row fall in the 8192 cache tokens of one index of seq, and in every row the cache of some index of seq holds exactly 4 of them. `slash_offsets`: entries of a row are distinct; the first entry of every row is 0.
All inputs are finite; a program needn't handle non-finite values.
Results may differ from the reference program's by a relative error of at most 0.0031.
Values may be sent and summed in bfloat16 or wider, within the bound.
No kernel may reach another device: no remote copies, remote signals or barrier semaphores. Data moves between devices by JAX's collectives and lax.ppermute only.
A program may use at most 128 MiB of HBM per device.

```python
import jax
import jax.numpy as jnp
from jax import lax

HQ = 64
HK = 8
HD = 128
BLK = 64
NS = 3
VPD = 1
VCAP = 4
QD = 512
CD = 8192
QTOT = 16384
CTOT = 262144
NV = 32


def draw_queries(key, part):
    shape_rows = (QTOT, HQ * HD)
    values = 2.5 * jax.random.truncated_normal(jax.random.fold_in(key, 1), -3.2, 3.2, shape_rows, jnp.float32)
    return values.astype(jnp.bfloat16)


def draw_new_kv(key, part):
    shape_rows = (2, QTOT, HK * HD)
    values = jax.random.truncated_normal(jax.random.fold_in(key, 2), -6.0, 6.0, shape_rows, jnp.float32)
    return values.astype(jnp.bfloat16)


def draw_vertical_blocks(key, part):
    owners = NV // VPD
    cache_blocks = CD // BLK
    qblocks = QD // BLK

    def one_row(row_key):
        row_keys = jax.random.split(row_key, 5)
        forced = jax.random.randint(row_keys[0], (), 0, owners)
        slot_ids = jnp.arange(owners * VCAP)
        slot_owner = slot_ids // VCAP
        ranking = jax.random.permutation(row_keys[1], owners * VCAP)
        score = jnp.where(slot_owner == forced, slot_ids - 2 * owners * VCAP, ranking)
        chosen = jnp.argsort(score)[:NV]
        owner_index = chosen // VCAP
        slot_index = chosen % VCAP
        spots = jax.vmap(lambda sub_key: jax.random.permutation(sub_key, cache_blocks))(jax.random.split(row_keys[2], owners))
        last_spots = jax.random.permutation(row_keys[3], cache_blocks - qblocks)
        block_pick = jnp.where(owner_index == owners - 1, last_spots[slot_index], spots[owner_index, slot_index])
        entries = owner_index * cache_blocks + block_pick
        return entries[jax.random.permutation(row_keys[4], NV)]
    return jax.vmap(one_row)(jax.random.split(key, HK)).astype(jnp.int32)


def draw_slash_offsets(key, part):
    qblocks = QD // BLK

    def one_row(row_key):
        return jax.random.permutation(row_key, qblocks - 1)[:NS - 1] + 1
    others = jax.vmap(one_row)(jax.random.split(jax.random.fold_in(key, 3), HQ))
    forced = jax.random.randint(jax.random.fold_in(key, 5), (), 0, HQ)
    present = jnp.any(others == qblocks - 1, axis=1)
    fixing = (jnp.arange(HQ) == forced) & jnp.logical_not(present)
    first_other = jnp.where(fixing, qblocks - 1, others[:, 0])
    zeros_col = jnp.zeros((HQ, 1), jnp.int32)
    return jnp.concatenate([zeros_col, first_other[:, None].astype(jnp.int32), others[:, 1:].astype(jnp.int32)], axis=1)


def levels(own_key, shape, cuts, smallest, largest):
    def one(dim, shards_of):
        draws = jax.random.uniform(jax.random.fold_in(jax.random.fold_in(own_key, 6), dim), (shards_of,), jnp.float32, smallest / len(cuts), largest / len(cuts))
        return jnp.repeat(jnp.exp(draws), shape[dim] // shards_of).reshape((-1,) + (1,) * (len(shape) - dim - 1))

    loudness = one(*cuts[0])
    for cut in cuts[1:]:
        loudness = loudness * one(*cut)
    return loudness


def gaussian(stream_key, shape, spread, most, cuts=(), held_as=jnp.bfloat16):
    values = spread * jax.random.normal(stream_key, shape, jnp.float32)
    if cuts:
        values = values * levels(stream_key, shape, cuts, -0.22, 0.18)
    return jnp.clip(values, -most, most).astype(held_as)


def setup_inputs(seed: int = 0) -> dict:
    arg_keys = jax.random.split(jax.random.key(seed), 6)
    return {
        "queries": draw_queries(jax.random.fold_in(arg_keys[5], 71), 0),
        "new_kv": draw_new_kv(jax.random.fold_in(arg_keys[5], 71), 0),
        "cache_kv": gaussian(arg_keys[2], (2, CTOT, HK * HD), 1.0, 6.0, ((1, 32), (2, 4))),
        "vertical_blocks": draw_vertical_blocks(jax.random.fold_in(arg_keys[5], 71), 0),
        "slash_offsets": draw_slash_offsets(jax.random.fold_in(arg_keys[5], 71), 0),
    }


NEG_FILL = -1e30


def reference(queries, new_kv, cache_kv, vertical_blocks, slash_offsets):
    group_size = HQ // HK
    qblocks = QD // BLK
    new_blocks = QTOT // BLK
    factor = HD ** -0.5
    window = jnp.concatenate([cache_kv[:, CTOT - QD:, :], new_kv], axis=1)
    query_heads = queries.reshape(QTOT, HQ, HD)
    causal_tok = jnp.arange(BLK)[None, :] <= jnp.arange(BLK)[:, None]

    def per_head(head_id):
        kv_head = (head_id // group_size).astype(jnp.int32)
        cache_head = lax.dynamic_slice_in_dim(cache_kv, kv_head * HD, HD, axis=2)
        window_head = lax.dynamic_slice_in_dim(window, kv_head * HD, HD, axis=2)
        window_head = window_head.reshape(2, qblocks + new_blocks, BLK, HD)
        query_rows = lax.dynamic_index_in_dim(query_heads, head_id, axis=1, keepdims=False)
        listed = jnp.take(vertical_blocks, kv_head, axis=0)
        token_index = (listed[:, None] * BLK + jnp.arange(BLK, dtype=jnp.int32)[None, :]).reshape(-1)
        vert_keys = jnp.take(cache_head[0], token_index, axis=0).astype(jnp.float32)
        vert_values = jnp.take(cache_head[1], token_index, axis=0).astype(jnp.float32)
        vert_scores = jnp.dot(query_rows.astype(jnp.float32), vert_keys.T, preferred_element_type=jnp.float32) * factor
        offsets_row = jnp.take(slash_offsets, head_id, axis=0)
        block_index = qblocks + jnp.arange(new_blocks, dtype=jnp.int32)[:, None] - offsets_row[None, :]
        near_keys = window_head[0][block_index].astype(jnp.float32)
        near_values = window_head[1][block_index].astype(jnp.float32)
        query_blocks = query_rows.reshape(new_blocks, BLK, HD).astype(jnp.float32)
        near_scores = jnp.einsum('bid,bnjd->binj', query_blocks, near_keys) * factor
        near_mask = (offsets_row[None, :, None] > 0) | causal_tok[:, None, :]
        near_scores = jnp.where(near_mask[None], near_scores, NEG_FILL)
        vert_grid = vert_scores.reshape(new_blocks, BLK, -1)
        row_peak = jnp.maximum(vert_grid.max(axis=2), near_scores.max(axis=(2, 3)))
        vert_weights = jnp.exp(vert_grid - row_peak[:, :, None])
        near_weights = jnp.exp(near_scores - row_peak[:, :, None, None])
        row_total = vert_weights.sum(axis=2) + near_weights.sum(axis=(2, 3))
        vert_probs = lax.optimization_barrier(vert_weights.astype(jnp.bfloat16)).astype(jnp.float32)
        near_probs = lax.optimization_barrier(near_weights.astype(jnp.bfloat16)).astype(jnp.float32)
        mixed_sum = jnp.dot(vert_probs.reshape(QTOT, -1), vert_values, preferred_element_type=jnp.float32)
        mixed_sum = mixed_sum + jnp.einsum('binj,bnjd->bid', near_probs, near_values).reshape(QTOT, HD)
        return (mixed_sum / row_total.reshape(QTOT)[:, None]).astype(jnp.bfloat16)

    per_heads = lax.map(per_head, jnp.arange(HQ, dtype=jnp.int32))
    return jnp.transpose(per_heads, (1, 0, 2)).reshape(QTOT, HQ * HD)
```

```python
import functools

import jax
import jax.numpy as jnp
from jax import lax
from jax.experimental import pallas as pl
from jax.experimental.pallas import tpu as pltpu
from jax.sharding import PartitionSpec as P

HD = 128
BLK = 64
KVL = 2
GROUP = 8
ROWS = 128
SIDE = 4
CACHE_BLOCKS = 128
NEG_FILL = -1e30
FACTOR = (HD**-0.5) * 1.4426950408889634
NT = (((1,), (1,)), ((), ()))
VM = pl.BlockSpec(memory_space=pltpu.VMEM)
SM = pl.BlockSpec(memory_space=pltpu.SMEM)
ANY = pl.BlockSpec(memory_space=pl.ANY)
SLOT = jax.ShapeDtypeStruct((KVL, 2, BLK, HD), jnp.bfloat16)


def along_x(block, d):
    return lax.ppermute(block, "seq", [(i, (i + 8 * d) % 32) for i in range(32)])


def along_y(block, d):
    return lax.ppermute(block, "seq", [(i, i // 8 * 8 + (i + 2 * d) % 8) for i in range(32)])


def other_core(block):
    return lax.ppermute(block, "seq", [(i, i ^ 1) for i in range(32)])


def along_z(block, d):
    return lax.ppermute(block, "kvh", [(i, (i + d) % SIDE) for i in range(SIDE)])


def pick_kernel(ids, order, cache, new_kv, tail, *refs):
    outs, sems, tail_sem = refs[:SIDE], refs[SIDE], refs[SIDE + 1]
    x, y, core = ids[0], ids[1], ids[2]
    mine = core * 16 + y * SIDE + x
    last = (x == SIDE - 1) & (y == SIDE - 1) & (core == 1)
    rows = tail.shape[1]
    from_cache = pltpu.make_async_copy(
        cache.at[:, cache.shape[1] - rows :, :], tail, tail_sem
    )
    from_new = pltpu.make_async_copy(new_kv, tail, tail_sem)

    @pl.when(last)
    def _():
        from_cache.start()

    @pl.when(jnp.logical_not(last))
    def _():
        from_new.start()

    for wait in (False, True):
        for d in range(SIDE):
            home_x = lax.rem(x + d, SIDE)
            for h in range(KVL):
                for q in range(8):
                    key = order[h, q * SIDE + home_x]

                    @pl.when(lax.shift_right_logical(key, 7) == mine)
                    def _():
                        row = pl.multiple_of((key & (CACHE_BLOCKS - 1)) * BLK, BLK)
                        for part in range(2):
                            copy = pltpu.make_async_copy(
                                cache.at[part, pl.ds(row, BLK), h * HD : (h + 1) * HD],
                                outs[d].at[h, part],
                                sems.at[d, h, part],
                            )
                            if wait:
                                copy.wait()
                            else:
                                copy.start()

    from_new.wait()


def to_y_kernel(ids, order, *refs):
    ins, outs, sems = refs[:SIDE], refs[SIDE : 2 * SIDE], refs[2 * SIDE]
    x, y, core = ids[0], ids[1], ids[2]
    for wait in (False, True):
        for d in range(SIDE):
            home_y = lax.rem(y + d, SIDE)
            for h in range(KVL):
                for j in range(2):
                    owner = lax.shift_right_logical(
                        order[h, SIDE * (home_y + SIDE * j) + x], 7
                    )
                    here = lax.shift_right_logical(owner, 2) == core * SIDE + y
                    step = (x - owner) & (SIDE - 1)
                    for i in range(SIDE):

                        @pl.when(here & (step == i))
                        def _():
                            copy = pltpu.make_async_copy(
                                ins[i].at[h], outs[d].at[h], sems.at[d, h]
                            )
                            if wait:
                                copy.wait()
                            else:
                                copy.start()


def home_kernel(ids, order, *refs):
    ins, keep, send, sems = refs[:SIDE], refs[SIDE], refs[SIDE + 1], refs[SIDE + 2]
    x, y, core = ids[0], ids[1], ids[2]
    for wait in (False, True):
        for h in range(KVL):
            for j in range(2):
                owner = lax.shift_right_logical(order[h, SIDE * (y + SIDE * j) + x], 7)
                here = lax.shift_right_logical(owner, 4) == core
                step = (y - lax.shift_right_logical(owner, 2)) & (SIDE - 1)
                for i in range(SIDE):
                    for to, place in ((keep, core == j), (send, core != j)):

                        @pl.when(here & (step == i) & place)
                        def _():
                            copy = pltpu.make_async_copy(
                                ins[i].at[h], to.at[h], sems.at[h, j]
                            )
                            if wait:
                                copy.wait()
                            else:
                                copy.start()


def attention_kernel(meta, slash, q_ref, vert_a, vert_b, prev, new, out_ref, k2, va, nk2, nva, *, heads):
    base = meta[0]
    ri = lax.broadcasted_iota(jnp.int32, (ROWS, ROWS), 0)
    ci = lax.broadcasted_iota(jnp.int32, (ROWS, ROWS), 1)
    same = (ri // BLK) == (ci // BLK)
    causal = same & (ci <= ri)
    half_rows = vert_a.shape[0] * BLK
    near_rows = prev.shape[1]
    va[:, HD:] = jnp.ones((2 * half_rows, HD), jnp.bfloat16)
    nva[:, HD:] = jnp.ones((2 * near_rows, HD), jnp.bfloat16)
    for kv in range(KVL):
        cols = slice(kv * HD, (kv + 1) * HD)
        for n, (vert, near) in enumerate(((vert_a, prev), (vert_b, new))):
            at = slice(n * half_rows, (n + 1) * half_rows)
            near_at = slice(n * near_rows, (n + 1) * near_rows)
            for half in range(2):
                k2[at, half * HD : (half + 1) * HD] = vert[:, kv, 0].reshape(half_rows, HD)
                nk2[near_at, half * HD : (half + 1) * HD] = near[0, :, cols]
            va[at, :HD] = vert[:, kv, 1].reshape(half_rows, HD)
            nva[near_at, :HD] = near[1, :, cols]
        for first in range(kv * GROUP, (kv + 1) * GROUP, heads):
            q2s = []
            for h in range(first, first + heads):
                scaled = q_ref[:, h * HD : (h + 1) * HD].astype(jnp.float32) * FACTOR
                hi = scaled.astype(jnp.bfloat16)
                lo = (scaled - hi.astype(jnp.float32)).astype(jnp.bfloat16)
                q2s.append(jnp.concatenate([hi, lo], axis=1))
            scores = lax.dot_general(
                jnp.concatenate(q2s, axis=0), k2[...], NT, preferred_element_type=jnp.float32
            )
            near_scores, starts = [], []
            for i, h in enumerate(range(first, first + heads)):
                row = []
                for j in range(slash.shape[1]):
                    start = pl.multiple_of(base - (slash[h, j] if j else 0) * BLK, BLK)
                    starts.append(start)
                    part = lax.dot_general(
                        q2s[i], nk2[pl.ds(start, ROWS), :], NT, preferred_element_type=jnp.float32
                    )
                    row.append(jnp.where(same if j else causal, part, NEG_FILL))
                near_scores.append(row)
            near_peak = [functools.reduce(jnp.maximum, r).max(axis=1, keepdims=True) for r in near_scores]
            peak = jnp.maximum(scores.max(axis=1, keepdims=True), jnp.concatenate(near_peak, axis=0))
            probs = jnp.exp2(scores - peak).astype(jnp.bfloat16)
            mixed = jnp.dot(probs, va[...], preferred_element_type=jnp.float32)
            for i, h in enumerate(range(first, first + heads)):
                rows = slice(i * ROWS, (i + 1) * ROWS)
                one = mixed[rows]
                for j, part in enumerate(near_scores[i]):
                    near_probs = jnp.exp2(part - peak[rows]).astype(jnp.bfloat16)
                    start = starts[i * len(near_scores[i]) + j]
                    one = one + jnp.dot(
                        near_probs, nva[pl.ds(start, ROWS), :], preferred_element_type=jnp.float32
                    )
                out_ref[:, h * HD : (h + 1) * HD] = (one[:, :HD] / one[:, HD:]).astype(jnp.bfloat16)


def attention(meta, slash, q, vert_a, vert_b, prev, new):
    keys = 2 * vert_a.shape[0] * BLK
    near = 2 * prev.shape[1]
    scores = q.shape[0] * KVL * GROUP * keys
    return pl.pallas_call(
        functools.partial(attention_kernel, heads=4),
        out_shape=jax.ShapeDtypeStruct(q.shape, jnp.bfloat16),
        in_specs=[SM, SM, VM, VM, VM, VM, VM],
        out_specs=VM,
        scratch_shapes=[pltpu.VMEM((keys, 2 * HD), jnp.bfloat16)] * 2
        + [pltpu.VMEM((near, 2 * HD), jnp.bfloat16)] * 2,
        compiler_params=pltpu.CompilerParams(vmem_limit_bytes=60 * 2**20),
        cost_estimate=pl.CostEstimate(
            flops=8 * scores * HD, bytes_accessed=2**22, transcendentals=scores
        ),
    )(meta, slash, q, vert_a, vert_b, prev, new)


def join_kernel(ids, *refs):
    ins, out, sems = refs[:SIDE], refs[SIDE], refs[SIDE + 1]
    width = ins[0].shape[1]
    copies = []
    for d in range(SIDE):
        at = pl.multiple_of(lax.rem(ids[3] + d, SIDE) * width, width)
        copies.append(pltpu.make_async_copy(ins[d], out.at[:, pl.ds(at, width)], sems.at[d]))
    for copy in copies:
        copy.start()
    for copy in copies:
        copy.wait()


def local(queries, new_kv, cache_kv, vertical_blocks, slash_offsets):
    seq, z = lax.axis_index("seq"), lax.axis_index("kvh")
    ids = jnp.stack([seq // 8, seq // 2 % SIDE, seq % 2, z]).astype(jnp.int32)
    owner = vertical_blocks // CACHE_BLOCKS
    key = (owner % 2 * 16 + owner // 2 % SIDE * SIDE + owner // 8) * CACHE_BLOCKS
    key = key + vertical_blocks % CACHE_BLOCKS
    place = jnp.sum(key[:, None, :] < key[:, :, None], axis=2)
    entries = key.shape[1]
    order = jnp.sum(
        jnp.where(place[:, :, None] == jnp.arange(entries)[None, None, :], key[:, :, None], 0), axis=1
    )
    width = queries.shape[1] // SIDE
    asked = [queries_of(queries, z, d, width) for d in range(SIDE)]

    tail, *picked = pl.pallas_call(
        pick_kernel,
        out_shape=[jax.ShapeDtypeStruct(new_kv.shape, jnp.bfloat16)] + [SLOT] * SIDE,
        in_specs=[SM, SM, ANY, ANY],
        out_specs=[ANY] * (SIDE + 1),
        scratch_shapes=[pltpu.SemaphoreType.DMA((SIDE, KVL, 2)), pltpu.SemaphoreType.DMA],
    )(ids, order, cache_kv, new_kv)
    got = [picked[0]] + [along_x(picked[d], d) for d in range(1, SIDE)]
    to_y = pl.pallas_call(
        to_y_kernel,
        out_shape=[SLOT] * SIDE,
        in_specs=[SM, SM] + [ANY] * SIDE,
        out_specs=[ANY] * SIDE,
        scratch_shapes=[pltpu.SemaphoreType.DMA((SIDE, KVL))],
    )(ids, order, *got)
    got = [to_y[0]] + [along_y(to_y[d], d) for d in range(1, SIDE)]
    keep, send = pl.pallas_call(
        home_kernel,
        out_shape=[SLOT] * 2,
        in_specs=[SM, SM] + [ANY] * SIDE,
        out_specs=[ANY] * 2,
        scratch_shapes=[pltpu.SemaphoreType.DMA((KVL, 2))],
    )(ids, order, *got)
    swapped = other_core(send)
    home = order[:, :]
    at = SIDE * (ids[1] + SIDE * ids[2]) + ids[0]
    home = lax.dynamic_slice_in_dim(home, at, 1, axis=1) // (16 * CACHE_BLOCKS)
    home = jnp.where((home == ids[2])[:, :, None, None], keep, swapped)
    column = jnp.stack([home] + [along_y(home, d) for d in range(1, SIDE)])
    plane = jnp.concatenate([column] + [along_x(column, d) for d in range(1, SIDE)])
    plane_b = other_core(plane)
    prev = lax.ppermute(tail, "seq", [(i, (i + 1) % 32) for i in range(32)])

    chunks = {0: asked[0]}
    for d in range(1, SIDE):
        chunks[d] = along_z(asked[d], d)
    answers = {}
    for d in (2, 1, 3, 0):
        meta = (new_kv.shape[1] + ROWS * ((z - d) % SIDE)).astype(jnp.int32).reshape(1)
        done = attention(meta, slash_offsets, chunks[d], plane, plane_b, prev, new_kv)
        answers[d] = along_z(done, SIDE - d) if d else done
    return pl.pallas_call(
        join_kernel,
        out_shape=jax.ShapeDtypeStruct(queries.shape, jnp.bfloat16),
        in_specs=[SM] + [ANY] * SIDE,
        out_specs=ANY,
        scratch_shapes=[pltpu.SemaphoreType.DMA((SIDE,))],
    )(ids, *[answers[d] for d in range(SIDE)])


def queries_of(queries, z, d, width):
    return lax.dynamic_slice_in_dim(queries, (z + d) % SIDE * width, width, axis=1)


def solution(mesh):
    in_specs = (
        P(("seq", "kvh"), None),
        P(None, "seq", "kvh"),
        P(None, "seq", "kvh"),
        P("kvh", None),
        P("kvh", None),
    )
    out_specs = P(("seq", "kvh"), None)
    return jax.shard_map(local, mesh=mesh, in_specs=in_specs, out_specs=out_specs, check_vma=False)
```

```python
import functools

import jax
import jax.numpy as jnp
from jax import lax
from jax.experimental import pallas as pl
from jax.experimental.pallas import tpu as pltpu
from jax.sharding import PartitionSpec as P

HD = 128
BLK = 64
KVL = 2
GROUP = 8
ROWS = 128
SIDE = 4
CACHE_BLOCKS = 128
NEG_FILL = -1e30
FACTOR = (HD**-0.5) * 1.4426950408889634
NT = (((1,), (1,)), ((), ()))
VM = pl.BlockSpec(memory_space=pltpu.VMEM)
SM = pl.BlockSpec(memory_space=pltpu.SMEM)
ANY = pl.BlockSpec(memory_space=pl.ANY)
SLOT = jax.ShapeDtypeStruct((KVL, 2, BLK, HD), jnp.bfloat16)


def along_x(block, d):
    return lax.ppermute(block, "seq", [(i, (i + 8 * d) % 32) for i in range(32)])


def along_y(block, d):
    return lax.ppermute(block, "seq", [(i, i // 8 * 8 + (i + 2 * d) % 8) for i in range(32)])


def other_core(block):
    return lax.ppermute(block, "seq", [(i, i ^ 1) for i in range(32)])


def along_z(block, d):
    return lax.ppermute(block, "kvh", [(i, (i + d) % SIDE) for i in range(SIDE)])


def pick_kernel(ids, order, cache, *refs):
    outs, sems = refs[:SIDE], refs[SIDE]
    x, y, core = ids[0], ids[1], ids[2]
    mine = core * 16 + y * SIDE + x
    for wait in (False, True):
        for d in range(SIDE):
            home_x = lax.rem(x + d, SIDE)
            for h in range(KVL):
                for q in range(8):
                    key = order[h, q * SIDE + home_x]

                    @pl.when(lax.shift_right_logical(key, 7) == mine)
                    def _():
                        row = pl.multiple_of((key & (CACHE_BLOCKS - 1)) * BLK, BLK)
                        for part in range(2):
                            copy = pltpu.make_async_copy(
                                cache.at[part, pl.ds(row, BLK), h * HD : (h + 1) * HD],
                                outs[d].at[h, part],
                                sems.at[d, h, part],
                            )
                            if wait:
                                copy.wait()
                            else:
                                copy.start()


def to_y_kernel(ids, order, *refs):
    ins, outs = refs[:SIDE], refs[SIDE:]
    x, y, core = ids[0], ids[1], ids[2]
    for d in range(SIDE):
        home_y = lax.rem(y + d, SIDE)
        for h in range(KVL):
            for j in range(2):
                owner = lax.shift_right_logical(order[h, SIDE * (home_y + SIDE * j) + x], 7)
                here = lax.shift_right_logical(owner, 2) == core * SIDE + y
                step = (x - owner) & (SIDE - 1)
                for i in range(SIDE):

                    @pl.when(here & (step == i))
                    def _():
                        outs[d][h] = ins[i][h]


def home_kernel(ids, order, *refs):
    ins, keep, send = refs[:SIDE], refs[SIDE], refs[SIDE + 1]
    x, y, core = ids[0], ids[1], ids[2]
    for h in range(KVL):
        for j in range(2):
            owner = lax.shift_right_logical(order[h, SIDE * (y + SIDE * j) + x], 7)
            here = lax.shift_right_logical(owner, 4) == core
            step = (y - lax.shift_right_logical(owner, 2)) & (SIDE - 1)
            for i in range(SIDE):
                for to, place in ((keep, core == j), (send, core != j)):

                    @pl.when(here & (step == i) & place)
                    def _():
                        to[h] = ins[i][h]


def attention_kernel(meta, slash, q_ref, vert_a, vert_b, prev, new, out_ref, va, nk, nva, *, heads):
    kv = pl.program_id(0)
    base = meta[0]
    ri = lax.broadcasted_iota(jnp.int32, (ROWS, ROWS), 0)
    ci = lax.broadcasted_iota(jnp.int32, (ROWS, ROWS), 1)
    same = (ri // BLK) == (ci // BLK)
    causal = same & (ci <= ri)
    half_rows = vert_a.shape[0] * BLK
    near_rows = prev.shape[1]
    va[:, HD:] = jnp.ones((2 * half_rows, HD), jnp.bfloat16)
    nva[:, HD:] = jnp.ones((2 * near_rows, HD), jnp.bfloat16)
    for n, (vert, near) in enumerate(((vert_a, prev), (vert_b, new))):
        va[n * half_rows : (n + 1) * half_rows, :HD] = vert[:, 0, 1].reshape(half_rows, HD)
        nk[n * near_rows : (n + 1) * near_rows, :] = near[0]
        nva[n * near_rows : (n + 1) * near_rows, :HD] = near[1]
    for first in range(0, GROUP, heads):
        group = range(first, first + heads)
        asked = [q_ref[0, :, h * HD : (h + 1) * HD] for h in group]
        rows_in = jnp.concatenate(asked, axis=0)
        scores = jnp.concatenate(
            [
                lax.dot_general(
                    rows_in, vert[:, 0, 0].reshape(half_rows, HD), NT, preferred_element_type=jnp.float32
                )
                for vert in (vert_a, vert_b)
            ],
            axis=1,
        )
        near_scores, starts = [], []
        for i, h in enumerate(group):
            row = []
            for j in range(slash.shape[1]):
                back = slash[kv * GROUP + h, j] if j else 0
                start = pl.multiple_of(base - back * BLK, BLK)
                starts.append(start)
                part = lax.dot_general(
                    asked[i], nk[pl.ds(start, ROWS), :], NT, preferred_element_type=jnp.float32
                )
                row.append(jnp.where(same if j else causal, part, NEG_FILL))
            near_scores.append(row)
        near_peak = [functools.reduce(jnp.maximum, r).max(axis=1, keepdims=True) for r in near_scores]
        peak = jnp.maximum(scores.max(axis=1, keepdims=True), jnp.concatenate(near_peak, axis=0))
        probs = jnp.exp2((scores - peak) * FACTOR).astype(jnp.bfloat16)
        mixed = jnp.dot(probs, va[...], preferred_element_type=jnp.float32)
        for i, h in enumerate(group):
            rows = slice(i * ROWS, (i + 1) * ROWS)
            one = mixed[rows]
            for j, part in enumerate(near_scores[i]):
                near_probs = jnp.exp2((part - peak[rows]) * FACTOR).astype(jnp.bfloat16)
                start = starts[i * len(near_scores[i]) + j]
                one = one + jnp.dot(
                    near_probs, nva[pl.ds(start, ROWS), :], preferred_element_type=jnp.float32
                )
            out_ref[:, h * HD : (h + 1) * HD] = (one[:, :HD] / one[:, HD:]).astype(jnp.bfloat16)


def attention(meta, slash, q, vert_a, vert_b, prev, new):
    entries, near = vert_a.shape[0], prev.shape[1]
    scores = ROWS * KVL * GROUP * 2 * entries * BLK
    vert_spec = pl.BlockSpec((entries, 1, 2, BLK, HD), lambda kv, meta: (0, kv, 0, 0, 0))
    near_spec = pl.BlockSpec((2, near, HD), lambda kv, meta: (0, 0, kv))
    return pl.pallas_call(
        functools.partial(attention_kernel, heads=2),
        grid_spec=pltpu.PrefetchScalarGridSpec(
            num_scalar_prefetch=1,
            grid=(KVL,),
            in_specs=[
                SM,
                pl.BlockSpec((1, ROWS, GROUP * HD), lambda kv, meta: (meta[1], 0, kv)),
                vert_spec,
                vert_spec,
                near_spec,
                near_spec,
            ],
            out_specs=pl.BlockSpec((ROWS, GROUP * HD), lambda kv, meta: (0, kv)),
            scratch_shapes=[
                pltpu.VMEM((2 * entries * BLK, 2 * HD), jnp.bfloat16),
                pltpu.VMEM((2 * near, HD), jnp.bfloat16),
                pltpu.VMEM((2 * near, 2 * HD), jnp.bfloat16),
            ],
        ),
        out_shape=jax.ShapeDtypeStruct(q.shape[1:], jnp.bfloat16),
        compiler_params=pltpu.CompilerParams(vmem_limit_bytes=56 * 2**20),
        cost_estimate=pl.CostEstimate(
            flops=8 * scores * HD, bytes_accessed=2**22, transcendentals=scores
        ),
    )(meta, slash, q, vert_a, vert_b, prev, new)


def join_kernel(ids, *refs):
    ins, out = refs[:SIDE], refs[SIDE]
    width = ins[0].shape[1]
    for d in range(SIDE):
        at = pl.multiple_of(lax.rem(ids[3] + d, SIDE) * width, width)
        out[:, pl.ds(at, width)] = ins[d][...]


def local(queries, new_kv, cache_kv, vertical_blocks, slash_offsets):
    seq, z = lax.axis_index("seq"), lax.axis_index("kvh")
    ids = jnp.stack([seq // 8, seq // 2 % SIDE, seq % 2, z]).astype(jnp.int32)
    owner = vertical_blocks // CACHE_BLOCKS
    key = (owner % 2 * 16 + owner // 2 % SIDE * SIDE + owner // 8) * CACHE_BLOCKS
    key = key + vertical_blocks % CACHE_BLOCKS
    place = jnp.sum(key[:, None, :] < key[:, :, None], axis=2)
    entries = key.shape[1]
    order = jnp.sum(
        jnp.where(place[:, :, None] == jnp.arange(entries)[None, None, :], key[:, :, None], 0), axis=1
    )
    width = queries.shape[1] // SIDE
    asked = jnp.stack([queries[:, i * width : (i + 1) * width] for i in range(SIDE)])
    asked = lax.all_to_all(asked, "kvh", split_axis=0, concat_axis=0, tiled=True)

    tail = jnp.where(seq == 31, cache_kv[:, cache_kv.shape[1] - new_kv.shape[1] :, :], new_kv)
    prev = lax.ppermute(tail, "seq", [(i, (i + 1) % 32) for i in range(32)])

    picked = pl.pallas_call(
        pick_kernel,
        out_shape=[SLOT] * SIDE,
        in_specs=[SM, SM, ANY],
        out_specs=[VM] * SIDE,
        scratch_shapes=[pltpu.SemaphoreType.DMA((SIDE, KVL, 2))],
    )(ids, order, cache_kv)
    got = [picked[0]] + [along_x(picked[d], d) for d in range(1, SIDE)]
    to_y = pl.pallas_call(
        to_y_kernel,
        out_shape=[SLOT] * SIDE,
        in_specs=[SM, SM] + [VM] * SIDE,
        out_specs=[VM] * SIDE,
    )(ids, order, *got)
    got = [to_y[0]] + [along_y(to_y[d], d) for d in range(1, SIDE)]
    keep, send = pl.pallas_call(
        home_kernel,
        out_shape=[SLOT] * 2,
        in_specs=[SM, SM] + [VM] * SIDE,
        out_specs=[VM] * 2,
    )(ids, order, *got)
    swapped = other_core(send)
    at = SIDE * (ids[1] + SIDE * ids[2]) + ids[0]
    home = lax.dynamic_slice_in_dim(order, at, 1, axis=1) // (16 * CACHE_BLOCKS)
    home = jnp.where((home == ids[2])[:, :, None, None], keep, swapped)
    column = jnp.stack([home] + [along_y(home, d) for d in range(1, SIDE)])
    column, asked, prev = lax.optimization_barrier((column, asked, prev))
    plane = jnp.concatenate([column] + [along_x(column, d) for d in range(1, SIDE)])
    plane_b = other_core(plane)

    answers = {}
    for d in (2, 1, 3, 0):
        source = (z - d) % SIDE
        meta = jnp.stack([new_kv.shape[1] + ROWS * source, source]).astype(jnp.int32)
        done = attention(meta, slash_offsets, asked, plane, plane_b, prev, new_kv)
        answers[d] = along_z(done, SIDE - d) if d else done
    return pl.pallas_call(
        join_kernel,
        out_shape=jax.ShapeDtypeStruct(queries.shape, jnp.bfloat16),
        in_specs=[SM] + [VM] * SIDE,
        out_specs=VM,
    )(ids, *[answers[d] for d in range(SIDE)])


def solution(mesh):
    in_specs = (
        P(("seq", "kvh"), None),
        P(None, "seq", "kvh"),
        P(None, "seq", "kvh"),
        P("kvh", None),
        P("kvh", None),
    )
    out_specs = P(("seq", "kvh"), None)
    return jax.shard_map(local, mesh=mesh, in_specs=in_specs, out_specs=out_specs, check_vma=False)
```

```python
import functools

import jax
import jax.numpy as jnp
from jax import lax
from jax.experimental import pallas as pl
from jax.experimental.pallas import tpu as pltpu
from jax.sharding import PartitionSpec as P

HD = 128
BLK = 64
KVL = 2
GROUP = 8
ROWS = 128
SIDE = 4
CACHE_BLOCKS = 128
NEG_FILL = -1e30
FACTOR = (HD**-0.5) * 1.4426950408889634
PIECE = 512
NT = (((1,), (1,)), ((), ()))
VM = pl.BlockSpec(memory_space=pltpu.VMEM)
SM = pl.BlockSpec(memory_space=pltpu.SMEM)
ANY = pl.BlockSpec(memory_space=pl.ANY)
SLOT = jax.ShapeDtypeStruct((KVL, 2, BLK, HD), jnp.bfloat16)


def along_x(block, d):
    return lax.ppermute(block, "seq", [(i, (i + 8 * d) % 32) for i in range(32)])


def along_y(block, d):
    return lax.ppermute(block, "seq", [(i, i // 8 * 8 + (i + 2 * d) % 8) for i in range(32)])


def other_core(block):
    return lax.ppermute(block, "seq", [(i, i ^ 1) for i in range(32)])


def along_z(block, d):
    return lax.ppermute(block, "kvh", [(i, (i + d) % SIDE) for i in range(SIDE)])


def pick_kernel(ids, order, cache, *refs):
    outs, sems = refs[:SIDE], refs[SIDE]
    x, y, core = ids[0], ids[1], ids[2]
    mine = core * 16 + y * SIDE + x
    for wait in (False, True):
        for d in range(SIDE):
            home_x = lax.rem(x + d, SIDE)
            for h in range(KVL):
                for q in range(8):
                    key = order[h, q * SIDE + home_x]

                    @pl.when(lax.shift_right_logical(key, 7) == mine)
                    def _():
                        row = pl.multiple_of((key & (CACHE_BLOCKS - 1)) * BLK, BLK)
                        for part in range(2):
                            copy = pltpu.make_async_copy(
                                cache.at[part, pl.ds(row, BLK), h * HD : (h + 1) * HD],
                                outs[d].at[h, part],
                                sems.at[d, h, part],
                            )
                            if wait:
                                copy.wait()
                            else:
                                copy.start()


def to_y_kernel(ids, order, *refs):
    ins, outs = refs[:SIDE], refs[SIDE:]
    x, y, core = ids[0], ids[1], ids[2]
    for d in range(SIDE):
        home_y = lax.rem(y + d, SIDE)
        for h in range(KVL):
            for j in range(2):
                owner = lax.shift_right_logical(order[h, SIDE * (home_y + SIDE * j) + x], 7)
                here = lax.shift_right_logical(owner, 2) == core * SIDE + y
                step = (x - owner) & (SIDE - 1)
                for i in range(SIDE):

                    @pl.when(here & (step == i))
                    def _():
                        outs[d][h] = ins[i][h]


def home_kernel(ids, order, *refs):
    ins, keep, send = refs[:SIDE], refs[SIDE], refs[SIDE + 1]
    x, y, core = ids[0], ids[1], ids[2]
    for h in range(KVL):
        for j in range(2):
            owner = lax.shift_right_logical(order[h, SIDE * (y + SIDE * j) + x], 7)
            here = lax.shift_right_logical(owner, 4) == core
            step = (y - lax.shift_right_logical(owner, 2)) & (SIDE - 1)
            for i in range(SIDE):
                for to, place in ((keep, core == j), (send, core != j)):

                    @pl.when(here & (step == i) & place)
                    def _():
                        to[h] = ins[i][h]


def attention_kernel(ids, slash, q_ref, vert_a, vert_b, prev, new, out_ref, va, nk, nva, *, back):
    half_rows, near_rows = vert_a.shape[0] * BLK, prev.shape[1]
    source = (ids[3] - back) & (SIDE - 1)
    base = pl.multiple_of(near_rows + source * ROWS, ROWS)
    ri = lax.broadcasted_iota(jnp.int32, (ROWS, ROWS), 0)
    ci = lax.broadcasted_iota(jnp.int32, (ROWS, ROWS), 1)
    same = (ri // BLK) == (ci // BLK)
    causal = same & (ci <= ri)
    va[:, HD:] = jnp.ones((2 * half_rows, HD), jnp.bfloat16)
    nva[:, HD:] = jnp.ones((2 * near_rows, HD), jnp.bfloat16)
    for kv in range(KVL):
        cols = slice(kv * HD, (kv + 1) * HD)
        for n, (vert, near) in enumerate(((vert_a, prev), (vert_b, new))):
            va[n * half_rows : (n + 1) * half_rows, :HD] = vert[:, kv, 1].reshape(half_rows, HD)
            nk[n * near_rows : (n + 1) * near_rows, :] = near[0, :, cols]
            nva[n * near_rows : (n + 1) * near_rows, :HD] = near[1, :, cols]
        for h in range(kv * GROUP, (kv + 1) * GROUP):
            asked = q_ref[source, :, h * HD : (h + 1) * HD]
            pieces = []
            for vert in (vert_a, vert_b):
                for at in range(0, vert.shape[0], PIECE // BLK):
                    keys = vert[at : at + PIECE // BLK, kv, 0].reshape(PIECE, HD)
                    pieces.append(lax.dot_general(asked, keys, NT, preferred_element_type=jnp.float32))
            starts, near_pieces = [], []
            for j in range(slash.shape[1]):
                start = base - slash[h, j] * BLK if j else base
                starts.append(pl.multiple_of(start, BLK))
                part = lax.dot_general(
                    asked, nk[pl.ds(starts[j], ROWS), :], NT, preferred_element_type=jnp.float32
                )
                near_pieces.append(jnp.where(same if j else causal, part, NEG_FILL))
            tiles = [p[:, c : c + HD] for p in pieces for c in range(0, PIECE, HD)]
            peak = functools.reduce(jnp.maximum, tiles + near_pieces).max(axis=1, keepdims=True)
            mixed = None
            for n, part in enumerate(pieces + near_pieces):
                probs = jnp.exp2((part - peak) * FACTOR).astype(jnp.bfloat16)
                if n < len(pieces):
                    values = va[n * PIECE : (n + 1) * PIECE, :]
                else:
                    values = nva[pl.ds(starts[n - len(pieces)], ROWS), :]
                one = jnp.dot(probs, values, preferred_element_type=jnp.float32)
                mixed = one if mixed is None else mixed + one
            out_ref[:, h * HD : (h + 1) * HD] = (mixed[:, :HD] / mixed[:, HD:]).astype(jnp.bfloat16)


def attention(ids, slash, q, vert_a, vert_b, prev, new, back):
    keys, near = 2 * vert_a.shape[0] * BLK, 2 * prev.shape[1]
    scores = ROWS * KVL * GROUP * keys
    return pl.pallas_call(
        functools.partial(attention_kernel, back=back),
        out_shape=jax.ShapeDtypeStruct(q.shape[1:], jnp.bfloat16),
        in_specs=[SM, SM] + [VM] * 5,
        out_specs=VM,
        scratch_shapes=[
            pltpu.VMEM((keys, 2 * HD), jnp.bfloat16),
            pltpu.VMEM((near, HD), jnp.bfloat16),
            pltpu.VMEM((near, 2 * HD), jnp.bfloat16),
        ],
        compiler_params=pltpu.CompilerParams(vmem_limit_bytes=20 * 2**20),
        cost_estimate=pl.CostEstimate(
            flops=8 * scores * HD, bytes_accessed=2**22, transcendentals=scores
        ),
    )(ids, slash, q, vert_a, vert_b, prev, new)


def split_kernel(rows, out):
    out[0] = rows[...]


def join_kernel(ids, *refs):
    ins, out = refs[:SIDE], refs[SIDE]
    width = ins[0].shape[1]
    for d in range(SIDE):
        at = pl.multiple_of(lax.rem(ids[3] + d, SIDE) * width, width)
        out[:, pl.ds(at, width)] = ins[d][...]


def local(queries, new_kv, cache_kv, vertical_blocks, slash_offsets):
    seq, z = lax.axis_index("seq"), lax.axis_index("kvh")
    ids = jnp.stack([seq // 8, seq // 2 % SIDE, seq % 2, z]).astype(jnp.int32)
    owner = vertical_blocks // CACHE_BLOCKS
    key = (owner % 2 * 16 + owner // 2 % SIDE * SIDE + owner // 8) * CACHE_BLOCKS
    key = key + vertical_blocks % CACHE_BLOCKS
    place = jnp.sum(key[:, None, :] < key[:, :, None], axis=2)
    entries = key.shape[1]
    order = jnp.sum(
        jnp.where(place[:, :, None] == jnp.arange(entries)[None, None, :], key[:, :, None], 0), axis=1
    )
    width = queries.shape[1] // SIDE
    asked = pl.pallas_call(
        split_kernel,
        grid=(SIDE,),
        out_shape=jax.ShapeDtypeStruct((SIDE, ROWS, width), jnp.bfloat16),
        in_specs=[pl.BlockSpec((ROWS, width), lambda i: (0, i))],
        out_specs=pl.BlockSpec((1, ROWS, width), lambda i: (i, 0, 0)),
        compiler_params=pltpu.CompilerParams(vmem_limit_bytes=8 * 2**20),
    )(queries)
    asked = lax.all_to_all(asked, "kvh", split_axis=0, concat_axis=0, tiled=True)

    tail = jnp.where(seq == 31, cache_kv[:, cache_kv.shape[1] - new_kv.shape[1] :, :], new_kv)
    prev = lax.ppermute(tail, "seq", [(i, (i + 1) % 32) for i in range(32)])

    picked = pl.pallas_call(
        pick_kernel,
        out_shape=[SLOT] * SIDE,
        in_specs=[SM, SM, ANY],
        out_specs=[VM] * SIDE,
        scratch_shapes=[pltpu.SemaphoreType.DMA((SIDE, KVL, 2))],
    )(ids, order, cache_kv)
    got = [picked[0]] + [along_x(picked[d], d) for d in range(1, SIDE)]
    to_y = pl.pallas_call(
        to_y_kernel,
        out_shape=[SLOT] * SIDE,
        in_specs=[SM, SM] + [VM] * SIDE,
        out_specs=[VM] * SIDE,
    )(ids, order, *got)
    got = [to_y[0]] + [along_y(to_y[d], d) for d in range(1, SIDE)]
    keep, send = pl.pallas_call(
        home_kernel,
        out_shape=[SLOT] * 2,
        in_specs=[SM, SM] + [VM] * SIDE,
        out_specs=[VM] * 2,
    )(ids, order, *got)
    swapped = other_core(send)
    at = SIDE * (ids[1] + SIDE * ids[2]) + ids[0]
    home = lax.dynamic_slice_in_dim(order, at, 1, axis=1) // (16 * CACHE_BLOCKS)
    home = jnp.where((home == ids[2])[:, :, None, None], keep, swapped)
    column = jnp.stack([home] + [along_y(home, d) for d in range(1, SIDE)])
    column, asked, prev, slash = lax.optimization_barrier((column, asked, prev, slash_offsets))
    plane = jnp.concatenate([column] + [along_x(column, d) for d in range(1, SIDE)])
    plane_b = other_core(plane)

    answers = {}
    for d in (2, 1, 3, 0):
        done = attention(ids, slash, asked, plane, plane_b, prev, new_kv, d)
        answers[d] = along_z(done, SIDE - d) if d else done
    return pl.pallas_call(
        join_kernel,
        out_shape=jax.ShapeDtypeStruct(queries.shape, jnp.bfloat16),
        in_specs=[SM] + [VM] * SIDE,
        out_specs=VM,
    )(ids, *[answers[d] for d in range(SIDE)])


def solution(mesh):
    in_specs = (
        P(("seq", "kvh"), None),
        P(None, "seq", "kvh"),
        P(None, "seq", "kvh"),
        P("kvh", None),
        P("kvh", None),
    )
    out_specs = P(("seq", "kvh"), None)
    return jax.shard_map(local, mesh=mesh, in_specs=in_specs, out_specs=out_specs, check_vma=False)
```

```python
import functools

import jax
import jax.numpy as jnp
from jax import lax
from jax.experimental import pallas as pl
from jax.experimental.pallas import tpu as pltpu
from jax.sharding import PartitionSpec as P

HD = 128
BLK = 64
KVL = 2
GROUP = 8
ROWS = 128
SIDE = 4
CACHE_BLOCKS = 128
NEG_FILL = -1e30
FACTOR = (HD**-0.5) * 1.4426950408889634
PIECE = 512
NT = (((1,), (1,)), ((), ()))
VM = pl.BlockSpec(memory_space=pltpu.VMEM)
SM = pl.BlockSpec(memory_space=pltpu.SMEM)
ANY = pl.BlockSpec(memory_space=pl.ANY)
SLOT = jax.ShapeDtypeStruct((KVL, 2, BLK, HD), jnp.bfloat16)


def along_x(block, d):
    return lax.ppermute(block, "seq", [(i, (i + 8 * d) % 32) for i in range(32)])


def along_y(block, d):
    return lax.ppermute(block, "seq", [(i, i // 8 * 8 + (i + 2 * d) % 8) for i in range(32)])


def other_core(block):
    return lax.ppermute(block, "seq", [(i, i ^ 1) for i in range(32)])


def along_z(block, d):
    return lax.ppermute(block, "kvh", [(i, (i + d) % SIDE) for i in range(SIDE)])


def pick_kernel(ids, order, cache, *refs):
    outs, sems = refs[:SIDE], refs[SIDE]
    x, y, core = ids[0], ids[1], ids[2]
    mine = core * 16 + y * SIDE + x
    for wait in (False, True):
        for d in range(SIDE):
            home_x = lax.rem(x + d, SIDE)
            for h in range(KVL):
                for q in range(8):
                    key = order[h, q * SIDE + home_x]

                    @pl.when(lax.shift_right_logical(key, 7) == mine)
                    def _():
                        row = pl.multiple_of((key & (CACHE_BLOCKS - 1)) * BLK, BLK)
                        for part in range(2):
                            copy = pltpu.make_async_copy(
                                cache.at[part, pl.ds(row, BLK), h * HD : (h + 1) * HD],
                                outs[d].at[h, part],
                                sems.at[d, h, part],
                            )
                            if wait:
                                copy.wait()
                            else:
                                copy.start()


def to_y_kernel(ids, order, *refs):
    ins, outs = refs[:SIDE], refs[SIDE:]
    x, y, core = ids[0], ids[1], ids[2]
    for d in range(SIDE):
        home_y = lax.rem(y + d, SIDE)
        for h in range(KVL):
            for j in range(2):
                owner = lax.shift_right_logical(order[h, SIDE * (home_y + SIDE * j) + x], 7)
                here = lax.shift_right_logical(owner, 2) == core * SIDE + y
                step = (x - owner) & (SIDE - 1)
                for i in range(SIDE):

                    @pl.when(here & (step == i))
                    def _():
                        outs[d][h] = ins[i][h]


def home_kernel(ids, order, *refs):
    ins, keep, send = refs[:SIDE], refs[SIDE], refs[SIDE + 1]
    x, y, core = ids[0], ids[1], ids[2]
    for h in range(KVL):
        for j in range(2):
            owner = lax.shift_right_logical(order[h, SIDE * (y + SIDE * j) + x], 7)
            here = lax.shift_right_logical(owner, 4) == core
            step = (y - lax.shift_right_logical(owner, 2)) & (SIDE - 1)
            for i in range(SIDE):
                for to, place in ((keep, core == j), (send, core != j)):

                    @pl.when(here & (step == i) & place)
                    def _():
                        to[h] = ins[i][h]


def attention_kernel(ids, slash, q_ref, prev, new, *refs, back):
    verts, (out_ref, va, nk, nva) = refs[:-4], refs[-4:]
    part_rows, near_rows = verts[0].shape[0] * BLK, prev.shape[1]
    source = (ids[3] - back) & (SIDE - 1)
    base = pl.multiple_of(near_rows + source * ROWS, ROWS)
    ri = lax.broadcasted_iota(jnp.int32, (ROWS, ROWS), 0)
    ci = lax.broadcasted_iota(jnp.int32, (ROWS, ROWS), 1)
    same = (ri // BLK) == (ci // BLK)
    causal = same & (ci <= ri)
    va[:, HD:] = jnp.ones((va.shape[0], HD), jnp.bfloat16)
    nva[:, HD:] = jnp.ones((2 * near_rows, HD), jnp.bfloat16)
    for kv in range(KVL):
        cols = slice(kv * HD, (kv + 1) * HD)
        for n, vert in enumerate(verts):
            va[n * part_rows : (n + 1) * part_rows, :HD] = vert[:, kv, 1].reshape(part_rows, HD)
        for n, near in enumerate((prev, new)):
            nk[n * near_rows : (n + 1) * near_rows, :] = near[0, :, cols]
            nva[n * near_rows : (n + 1) * near_rows, :HD] = near[1, :, cols]
        for h in range(kv * GROUP, (kv + 1) * GROUP):
            asked = q_ref[source, :, h * HD : (h + 1) * HD]
            pieces = []
            joined = PIECE // part_rows
            for n in range(0, len(verts), joined):
                keys = [vert[:, kv, 0].reshape(part_rows, HD) for vert in verts[n : n + joined]]
                keys = jnp.concatenate(keys, axis=0)
                pieces.append(lax.dot_general(asked, keys, NT, preferred_element_type=jnp.float32))
            starts, near_pieces = [], []
            for j in range(slash.shape[1]):
                start = base - slash[h, j] * BLK if j else base
                starts.append(pl.multiple_of(start, BLK))
                part = lax.dot_general(
                    asked, nk[pl.ds(starts[j], ROWS), :], NT, preferred_element_type=jnp.float32
                )
                near_pieces.append(jnp.where(same if j else causal, part, NEG_FILL))
            tiles = [p[:, c : c + HD] for p in pieces for c in range(0, PIECE, HD)]
            peak = functools.reduce(jnp.maximum, tiles + near_pieces).max(axis=1, keepdims=True)
            mixed = None
            for n, part in enumerate(pieces + near_pieces):
                probs = jnp.exp2((part - peak) * FACTOR).astype(jnp.bfloat16)
                if n < len(pieces):
                    values = va[n * PIECE : (n + 1) * PIECE, :]
                else:
                    values = nva[pl.ds(starts[n - len(pieces)], ROWS), :]
                one = jnp.dot(probs, values, preferred_element_type=jnp.float32)
                mixed = one if mixed is None else mixed + one
            out_ref[:, h * HD : (h + 1) * HD] = (mixed[:, :HD] / mixed[:, HD:]).astype(jnp.bfloat16)


def attention(ids, slash, q, prev, new, verts, back):
    keys, near = len(verts) * verts[0].shape[0] * BLK, 2 * prev.shape[1]
    scores = ROWS * KVL * GROUP * keys
    return pl.pallas_call(
        functools.partial(attention_kernel, back=back),
        out_shape=jax.ShapeDtypeStruct(q.shape[1:], jnp.bfloat16),
        in_specs=[SM, SM] + [VM] * (3 + len(verts)),
        out_specs=VM,
        scratch_shapes=[
            pltpu.VMEM((keys, 2 * HD), jnp.bfloat16),
            pltpu.VMEM((near, HD), jnp.bfloat16),
            pltpu.VMEM((near, 2 * HD), jnp.bfloat16),
        ],
        compiler_params=pltpu.CompilerParams(vmem_limit_bytes=20 * 2**20),
        cost_estimate=pl.CostEstimate(
            flops=8 * scores * HD, bytes_accessed=2**22, transcendentals=scores
        ),
    )(ids, slash, q, prev, new, *verts)


def split_kernel(rows, out):
    out[0] = rows[...]


def join_kernel(ids, *refs, steps):
    ins, out, sems = refs[: len(steps)], refs[-2], refs[-1]
    width = ins[0].shape[1]
    copies = []
    for n, d in enumerate(steps):
        at = pl.multiple_of(((ids[3] + d) & (SIDE - 1)) * width, width)
        copies.append(pltpu.make_async_copy(ins[n], out.at[:, pl.ds(at, width)], sems.at[n]))
    for copy in copies:
        copy.start()
    for copy in copies:
        copy.wait()


def join(ids, answers, steps, shape, onto=None):
    given = [] if onto is None else [onto]
    return pl.pallas_call(
        functools.partial(join_kernel, steps=steps),
        out_shape=jax.ShapeDtypeStruct(shape, jnp.bfloat16),
        in_specs=[SM] + [VM] * len(steps) + [ANY] * len(given),
        out_specs=ANY,
        scratch_shapes=[pltpu.SemaphoreType.DMA((len(steps),))],
        input_output_aliases={1 + len(steps): 0} if given else {},
        compiler_params=pltpu.CompilerParams(vmem_limit_bytes=8 * 2**20),
    )(ids, *[answers[d] for d in steps], *given)


def local(queries, new_kv, cache_kv, vertical_blocks, slash_offsets):
    seq, z = lax.axis_index("seq"), lax.axis_index("kvh")
    ids = jnp.stack([seq // 8, seq // 2 % SIDE, seq % 2, z]).astype(jnp.int32)
    owner = vertical_blocks // CACHE_BLOCKS
    key = (owner % 2 * 16 + owner // 2 % SIDE * SIDE + owner // 8) * CACHE_BLOCKS
    key = key + vertical_blocks % CACHE_BLOCKS
    place = jnp.sum(key[:, None, :] < key[:, :, None], axis=2)
    entries = key.shape[1]
    order = jnp.sum(
        jnp.where(place[:, :, None] == jnp.arange(entries)[None, None, :], key[:, :, None], 0), axis=1
    )
    width = queries.shape[1] // SIDE
    asked = pl.pallas_call(
        split_kernel,
        grid=(SIDE,),
        out_shape=jax.ShapeDtypeStruct((SIDE, ROWS, width), jnp.bfloat16),
        in_specs=[pl.BlockSpec((ROWS, width), lambda i: (0, i))],
        out_specs=pl.BlockSpec((1, ROWS, width), lambda i: (i, 0, 0)),
        compiler_params=pltpu.CompilerParams(vmem_limit_bytes=8 * 2**20),
    )(queries)
    asked = lax.all_to_all(asked, "kvh", split_axis=0, concat_axis=0, tiled=True)

    tail = jnp.where(seq == 31, cache_kv[:, cache_kv.shape[1] - new_kv.shape[1] :, :], new_kv)
    prev = lax.ppermute(tail, "seq", [(i, (i + 1) % 32) for i in range(32)])

    picked = pl.pallas_call(
        pick_kernel,
        out_shape=[SLOT] * SIDE,
        in_specs=[SM, SM, ANY],
        out_specs=[VM] * SIDE,
        scratch_shapes=[pltpu.SemaphoreType.DMA((SIDE, KVL, 2))],
    )(ids, order, cache_kv)
    got = [picked[0]] + [along_x(picked[d], d) for d in range(1, SIDE)]
    to_y = pl.pallas_call(
        to_y_kernel,
        out_shape=[SLOT] * SIDE,
        in_specs=[SM, SM] + [VM] * SIDE,
        out_specs=[VM] * SIDE,
    )(ids, order, *got)
    got = [to_y[0]] + [along_y(to_y[d], d) for d in range(1, SIDE)]
    keep, send = pl.pallas_call(
        home_kernel,
        out_shape=[SLOT] * 2,
        in_specs=[SM, SM] + [VM] * SIDE,
        out_specs=[VM] * 2,
    )(ids, order, *got)
    swapped = other_core(send)
    at = SIDE * (ids[1] + SIDE * ids[2]) + ids[0]
    home = lax.dynamic_slice_in_dim(order, at, 1, axis=1) // (16 * CACHE_BLOCKS)
    home = jnp.where((home == ids[2])[:, :, None, None], keep, swapped)
    column = jnp.stack([home] + [along_y(home, d) for d in range(1, SIDE)])
    column, asked, prev, slash = lax.optimization_barrier((column, asked, prev, slash_offsets))
    plane = [column] + [along_x(column, d) for d in range(1, SIDE)]
    plane += [other_core(part) for part in plane]

    answers = {}
    for d in (2, 1, 3, 0):
        done = attention(ids, slash, asked, prev, new_kv, plane, d)
        answers[d] = along_z(done, SIDE - d) if d else done
    first = join(ids, answers, (0, 1, 2), queries.shape)
    return join(ids, answers, (3,), queries.shape, first)


def solution(mesh):
    in_specs = (
        P(("seq", "kvh"), None),
        P(None, "seq", "kvh"),
        P(None, "seq", "kvh"),
        P("kvh", None),
        P("kvh", None),
    )
    out_specs = P(("seq", "kvh"), None)
    return jax.shard_map(local, mesh=mesh, in_specs=in_specs, out_specs=out_specs, check_vma=False)
```

```python
import functools

import jax
import jax.numpy as jnp
from jax import lax
from jax.experimental import pallas as pl
from jax.experimental.pallas import tpu as pltpu
from jax.sharding import PartitionSpec as P

HD = 128
BLK = 64
KVL = 2
GROUP = 8
ROWS = 128
SIDE = 4
CACHE_BLOCKS = 128
NEG_FILL = -1e30
FACTOR = (HD**-0.5) * 1.4426950408889634
PIECE = 512
NT = (((1,), (1,)), ((), ()))
VM = pl.BlockSpec(memory_space=pltpu.VMEM)
SM = pl.BlockSpec(memory_space=pltpu.SMEM)
ANY = pl.BlockSpec(memory_space=pl.ANY)
SLOT = jax.ShapeDtypeStruct((KVL, 2, BLK, HD), jnp.bfloat16)


def along_x(block, d):
    return lax.ppermute(block, "seq", [(i, (i + 8 * d) % 32) for i in range(32)])


def along_y(block, d):
    return lax.ppermute(block, "seq", [(i, i // 8 * 8 + (i + 2 * d) % 8) for i in range(32)])


def other_core(block):
    return lax.ppermute(block, "seq", [(i, i ^ 1) for i in range(32)])


def along_z(block, d):
    return lax.ppermute(block, "kvh", [(i, (i + d) % SIDE) for i in range(SIDE)])


def pick_kernel(ids, order, cache, *refs):
    outs, sems = refs[:SIDE], refs[SIDE]
    x, y, core = ids[0], ids[1], ids[2]
    mine = core * 16 + y * SIDE + x
    for wait in (False, True):
        for d in range(SIDE):
            home_x = lax.rem(x + d, SIDE)
            for h in range(KVL):
                for q in range(8):
                    key = order[h, q * SIDE + home_x]

                    @pl.when(lax.shift_right_logical(key, 7) == mine)
                    def _():
                        row = pl.multiple_of((key & (CACHE_BLOCKS - 1)) * BLK, BLK)
                        for part in range(2):
                            copy = pltpu.make_async_copy(
                                cache.at[part, pl.ds(row, BLK), h * HD : (h + 1) * HD],
                                outs[d].at[h, part],
                                sems.at[d, h, part],
                            )
                            if wait:
                                copy.wait()
                            else:
                                copy.start()


def to_y_kernel(ids, order, *refs):
    ins, outs = refs[:SIDE], refs[SIDE:]
    x, y, core = ids[0], ids[1], ids[2]
    for d in range(SIDE):
        home_y = lax.rem(y + d, SIDE)
        for h in range(KVL):
            for j in range(2):
                owner = lax.shift_right_logical(order[h, SIDE * (home_y + SIDE * j) + x], 7)
                here = lax.shift_right_logical(owner, 2) == core * SIDE + y
                step = (x - owner) & (SIDE - 1)
                for i in range(SIDE):

                    @pl.when(here & (step == i))
                    def _():
                        outs[d][h] = ins[i][h]


def home_kernel(ids, order, *refs):
    ins, keep, send = refs[:SIDE], refs[SIDE], refs[SIDE + 1]
    x, y, core = ids[0], ids[1], ids[2]
    for h in range(KVL):
        for j in range(2):
            owner = lax.shift_right_logical(order[h, SIDE * (y + SIDE * j) + x], 7)
            here = lax.shift_right_logical(owner, 4) == core
            step = (y - lax.shift_right_logical(owner, 2)) & (SIDE - 1)
            for i in range(SIDE):
                for to, place in ((keep, core == j), (send, core != j)):

                    @pl.when(here & (step == i) & place)
                    def _():
                        to[h] = ins[i][h]


def attention_kernel(ids, slash, q_ref, prev, new, *refs, back, heads_of):
    verts, (out_ref, va, nk, nva) = refs[:-4], refs[-4:]
    part_rows, near_rows = verts[0].shape[0] * BLK, prev.shape[1]
    source = (ids[3] - back) & (SIDE - 1)
    base = pl.multiple_of(near_rows + source * ROWS, ROWS)
    ri = lax.broadcasted_iota(jnp.int32, (ROWS, ROWS), 0)
    ci = lax.broadcasted_iota(jnp.int32, (ROWS, ROWS), 1)
    same = (ri // BLK) == (ci // BLK)
    causal = same & (ci <= ri)
    va[:, HD:] = jnp.ones((va.shape[0], HD), jnp.bfloat16)
    nva[:, HD:] = jnp.ones((2 * near_rows, HD), jnp.bfloat16)
    for kv in heads_of:
        cols = slice(kv * HD, (kv + 1) * HD)
        for n, vert in enumerate(verts):
            va[n * part_rows : (n + 1) * part_rows, :HD] = vert[:, kv, 1].reshape(part_rows, HD)
        for n, near in enumerate((prev, new)):
            nk[n * near_rows : (n + 1) * near_rows, :] = near[0, :, cols]
            nva[n * near_rows : (n + 1) * near_rows, :HD] = near[1, :, cols]
        for h in range(kv * GROUP, (kv + 1) * GROUP):
            asked = q_ref[source, :, h * HD : (h + 1) * HD]
            pieces = []
            joined = PIECE // part_rows
            for n in range(0, len(verts), joined):
                keys = [vert[:, kv, 0].reshape(part_rows, HD) for vert in verts[n : n + joined]]
                keys = jnp.concatenate(keys, axis=0)
                pieces.append(lax.dot_general(asked, keys, NT, preferred_element_type=jnp.float32))
            starts, near_pieces = [], []
            for j in range(slash.shape[1]):
                start = base - slash[h, j] * BLK if j else base
                starts.append(pl.multiple_of(start, BLK))
                part = lax.dot_general(
                    asked, nk[pl.ds(starts[j], ROWS), :], NT, preferred_element_type=jnp.float32
                )
                near_pieces.append(jnp.where(same if j else causal, part, NEG_FILL))
            tiles = [p[:, c : c + HD] for p in pieces for c in range(0, PIECE, HD)]
            peak = functools.reduce(jnp.maximum, tiles + near_pieces).max(axis=1, keepdims=True)
            mixed = None
            for n, part in enumerate(pieces + near_pieces):
                probs = jnp.exp2((part - peak) * FACTOR).astype(jnp.bfloat16)
                if n < len(pieces):
                    values = va[n * PIECE : (n + 1) * PIECE, :]
                else:
                    values = nva[pl.ds(starts[n - len(pieces)], ROWS), :]
                one = jnp.dot(probs, values, preferred_element_type=jnp.float32)
                mixed = one if mixed is None else mixed + one
            at = (h - heads_of[0] * GROUP) * HD
            out_ref[:, at : at + HD] = (mixed[:, :HD] / mixed[:, HD:]).astype(jnp.bfloat16)


def attention(ids, slash, q, prev, new, verts, back, heads_of=tuple(range(KVL))):
    keys, near = len(verts) * verts[0].shape[0] * BLK, 2 * prev.shape[1]
    scores = ROWS * len(heads_of) * GROUP * keys
    return pl.pallas_call(
        functools.partial(attention_kernel, back=back, heads_of=heads_of),
        out_shape=jax.ShapeDtypeStruct((ROWS, len(heads_of) * GROUP * HD), jnp.bfloat16),
        in_specs=[SM, SM] + [VM] * (3 + len(verts)),
        out_specs=VM,
        scratch_shapes=[
            pltpu.VMEM((keys, 2 * HD), jnp.bfloat16),
            pltpu.VMEM((near, HD), jnp.bfloat16),
            pltpu.VMEM((near, 2 * HD), jnp.bfloat16),
        ],
        compiler_params=pltpu.CompilerParams(vmem_limit_bytes=20 * 2**20),
        cost_estimate=pl.CostEstimate(
            flops=8 * scores * HD, bytes_accessed=2**22, transcendentals=scores
        ),
    )(ids, slash, q, prev, new, *verts)


def split_kernel(rows, out, sems):
    width = out.shape[2]
    copies = [
        pltpu.make_async_copy(rows.at[:, i * width : (i + 1) * width], out.at[i], sems.at[i])
        for i in range(SIDE)
    ]
    for copy in copies:
        copy.start()
    for copy in copies:
        copy.wait()


def join_kernel(ids, *refs, steps):
    ins, out, sems = refs[: len(steps)], refs[-2], refs[-1]
    width = KVL * GROUP * HD
    copies = []
    for n, (d, kv) in enumerate(steps):
        at = ((ids[3] + d) & (SIDE - 1)) * width + kv * GROUP * HD
        at = pl.multiple_of(at, GROUP * HD)
        copies.append(pltpu.make_async_copy(ins[n], out.at[:, pl.ds(at, ins[n].shape[1])], sems.at[n]))
    for copy in copies:
        copy.start()
    for copy in copies:
        copy.wait()


def join(ids, answers, steps, shape):
    return pl.pallas_call(
        functools.partial(join_kernel, steps=steps),
        out_shape=jax.ShapeDtypeStruct(shape, jnp.bfloat16),
        in_specs=[SM] + [VM] * len(steps),
        out_specs=ANY,
        scratch_shapes=[pltpu.SemaphoreType.DMA((len(steps),))],
        compiler_params=pltpu.CompilerParams(vmem_limit_bytes=8 * 2**20),
    )(ids, *[answers[step] for step in steps])


def local(queries, new_kv, cache_kv, vertical_blocks, slash_offsets):
    seq, z = lax.axis_index("seq"), lax.axis_index("kvh")
    ids = jnp.stack([seq // 8, seq // 2 % SIDE, seq % 2, z]).astype(jnp.int32)
    owner = vertical_blocks // CACHE_BLOCKS
    key = (owner % 2 * 16 + owner // 2 % SIDE * SIDE + owner // 8) * CACHE_BLOCKS
    key = key + vertical_blocks % CACHE_BLOCKS
    place = jnp.sum(key[:, None, :] < key[:, :, None], axis=2)
    entries = key.shape[1]
    order = jnp.sum(
        jnp.where(place[:, :, None] == jnp.arange(entries)[None, None, :], key[:, :, None], 0), axis=1
    )
    width = queries.shape[1] // SIDE
    asked = pl.pallas_call(
        split_kernel,
        out_shape=jax.ShapeDtypeStruct((SIDE, ROWS, width), jnp.bfloat16),
        in_specs=[ANY],
        out_specs=VM,
        scratch_shapes=[pltpu.SemaphoreType.DMA((SIDE,))],
        compiler_params=pltpu.CompilerParams(vmem_limit_bytes=60 * 2**20),
    )(queries)
    asked = lax.all_to_all(asked, "kvh", split_axis=0, concat_axis=0, tiled=True)

    tail = jnp.where(seq == 31, cache_kv[:, cache_kv.shape[1] - new_kv.shape[1] :, :], new_kv)

    picked = pl.pallas_call(
        pick_kernel,
        out_shape=[SLOT] * SIDE,
        in_specs=[SM, SM, ANY],
        out_specs=[VM] * SIDE,
        scratch_shapes=[pltpu.SemaphoreType.DMA((SIDE, KVL, 2))],
    )(ids, order, cache_kv)
    got = [picked[0]] + [along_x(picked[d], d) for d in range(1, SIDE)]
    to_y = pl.pallas_call(
        to_y_kernel,
        out_shape=[SLOT] * SIDE,
        in_specs=[SM, SM] + [VM] * SIDE,
        out_specs=[VM] * SIDE,
    )(ids, order, *got)
    got = [to_y[0]] + [along_y(to_y[d], d) for d in range(1, SIDE)]
    keep, send = pl.pallas_call(
        home_kernel,
        out_shape=[SLOT] * 2,
        in_specs=[SM, SM] + [VM] * SIDE,
        out_specs=[VM] * 2,
    )(ids, order, *got)
    swapped = other_core(send)
    at = SIDE * (ids[1] + SIDE * ids[2]) + ids[0]
    home = lax.dynamic_slice_in_dim(order, at, 1, axis=1) // (16 * CACHE_BLOCKS)
    home = jnp.where((home == ids[2])[:, :, None, None], keep, swapped)
    column = jnp.stack([home] + [along_y(home, d) for d in range(1, SIDE)])
    column, asked, tail, slash = lax.optimization_barrier((column, asked, tail, slash_offsets))
    plane = [column] + [along_x(column, d) for d in range(1, SIDE)]
    plane += [other_core(part) for part in plane]
    prev = lax.ppermute(tail, "seq", [(i, (i + 1) % 32) for i in range(32)])

    answers = {}
    for d, kvs in ((2, (0, 1)), (1, (0, 1)), (3, (0,)), (3, (1,)), (0, (0, 1))):
        done = attention(ids, slash, asked, prev, new_kv, plane, d, kvs)
        answers[d, kvs[0]] = along_z(done, SIDE - d) if d else done
    return join(ids, answers, ((0, 0), (1, 0), (2, 0), (3, 0), (3, 1)), queries.shape)


def solution(mesh):
    in_specs = (
        P(("seq", "kvh"), None),
        P(None, "seq", "kvh"),
        P(None, "seq", "kvh"),
        P("kvh", None),
        P("kvh", None),
    )
    out_specs = P(("seq", "kvh"), None)
    return jax.shard_map(local, mesh=mesh, in_specs=in_specs, out_specs=out_specs, check_vma=False)
```

```python
import functools

import jax
import jax.numpy as jnp
from jax import lax
from jax.experimental import pallas as pl
from jax.experimental.pallas import tpu as pltpu
from jax.sharding import PartitionSpec as P

HD = 128
BLK = 64
KVL = 2
GROUP = 8
ROWS = 128
SIDE = 4
CACHE_BLOCKS = 128
NEG_FILL = -1e30
FACTOR = (HD**-0.5) * 1.4426950408889634
PIECE = 512
NT = (((1,), (1,)), ((), ()))
VM = pl.BlockSpec(memory_space=pltpu.VMEM)
SM = pl.BlockSpec(memory_space=pltpu.SMEM)
ANY = pl.BlockSpec(memory_space=pl.ANY)
SLOT = jax.ShapeDtypeStruct((KVL, 2, BLK, HD), jnp.bfloat16)


def along_x(block, d):
    return lax.ppermute(block, "seq", [(i, (i + 8 * d) % 32) for i in range(32)])


def along_y(block, d):
    return lax.ppermute(block, "seq", [(i, i // 8 * 8 + (i + 2 * d) % 8) for i in range(32)])


def other_core(block):
    return lax.ppermute(block, "seq", [(i, i ^ 1) for i in range(32)])


def along_z(block, d):
    return lax.ppermute(block, "kvh", [(i, (i + d) % SIDE) for i in range(SIDE)])


def pick_kernel(ids, order, cache, *refs):
    outs, sems = refs[:SIDE], refs[SIDE]
    x, y, core = ids[0], ids[1], ids[2]
    mine = core * 16 + y * SIDE + x
    for wait in (False, True):
        for d in range(SIDE):
            home_x = lax.rem(x + d, SIDE)
            for h in range(KVL):
                for q in range(8):
                    key = order[h, q * SIDE + home_x]

                    @pl.when(lax.shift_right_logical(key, 7) == mine)
                    def _():
                        row = pl.multiple_of((key & (CACHE_BLOCKS - 1)) * BLK, BLK)
                        for part in range(2):
                            copy = pltpu.make_async_copy(
                                cache.at[part, pl.ds(row, BLK), h * HD : (h + 1) * HD],
                                outs[d].at[h, part],
                                sems.at[d, h, part],
                            )
                            if wait:
                                copy.wait()
                            else:
                                copy.start()


def to_y_kernel(ids, order, *refs):
    ins, outs = refs[:SIDE], refs[SIDE:]
    x, y, core = ids[0], ids[1], ids[2]
    for d in range(SIDE):
        home_y = lax.rem(y + d, SIDE)
        for h in range(KVL):
            for j in range(2):
                owner = lax.shift_right_logical(order[h, SIDE * (home_y + SIDE * j) + x], 7)
                here = lax.shift_right_logical(owner, 2) == core * SIDE + y
                step = (x - owner) & (SIDE - 1)
                for i in range(SIDE):

                    @pl.when(here & (step == i))
                    def _():
                        outs[d][h] = ins[i][h]


def home_kernel(ids, order, *refs):
    ins, keep, send = refs[:SIDE], refs[SIDE], refs[SIDE + 1]
    x, y, core = ids[0], ids[1], ids[2]
    for h in range(KVL):
        for j in range(2):
            owner = lax.shift_right_logical(order[h, SIDE * (y + SIDE * j) + x], 7)
            here = lax.shift_right_logical(owner, 4) == core
            step = (y - lax.shift_right_logical(owner, 2)) & (SIDE - 1)
            for i in range(SIDE):
                for to, place in ((keep, core == j), (send, core != j)):

                    @pl.when(here & (step == i) & place)
                    def _():
                        to[h] = ins[i][h]


def attention_kernel(ids, slash, q_ref, prev, new, *refs, back, heads_of):
    verts, (out_ref, va, nk, nva) = refs[:-4], refs[-4:]
    part_rows, near_rows = verts[0].shape[0] * BLK, prev.shape[1]
    source = (ids[3] - back) & (SIDE - 1)
    base = pl.multiple_of(near_rows + source * ROWS, ROWS)
    ri = lax.broadcasted_iota(jnp.int32, (ROWS, ROWS), 0)
    ci = lax.broadcasted_iota(jnp.int32, (ROWS, ROWS), 1)
    same = (ri // BLK) == (ci // BLK)
    causal = same & (ci <= ri)
    va[:, HD:] = jnp.ones((va.shape[0], HD), jnp.bfloat16)
    nva[:, HD:] = jnp.ones((2 * near_rows, HD), jnp.bfloat16)
    for kv in heads_of:
        cols = slice(kv * HD, (kv + 1) * HD)
        for n, vert in enumerate(verts):
            va[n * part_rows : (n + 1) * part_rows, :HD] = vert[:, kv, 1].reshape(part_rows, HD)
        for n, near in enumerate((prev, new)):
            nk[n * near_rows : (n + 1) * near_rows, :] = near[0, :, cols]
            nva[n * near_rows : (n + 1) * near_rows, :HD] = near[1, :, cols]
        for h in range(kv * GROUP, (kv + 1) * GROUP):
            asked = q_ref[source, :, h * HD : (h + 1) * HD]
            pieces = []
            joined = PIECE // part_rows
            for n in range(0, len(verts), joined):
                keys = [vert[:, kv, 0].reshape(part_rows, HD) for vert in verts[n : n + joined]]
                keys = jnp.concatenate(keys, axis=0)
                pieces.append(lax.dot_general(asked, keys, NT, preferred_element_type=jnp.float32))
            starts, near_pieces = [], []
            for j in range(slash.shape[1]):
                start = base - slash[h, j] * BLK if j else base
                starts.append(pl.multiple_of(start, BLK))
                part = lax.dot_general(
                    asked, nk[pl.ds(starts[j], ROWS), :], NT, preferred_element_type=jnp.float32
                )
                near_pieces.append(jnp.where(same if j else causal, part, NEG_FILL))
            tiles = [p[:, c : c + HD] for p in pieces for c in range(0, PIECE, HD)]
            peak = functools.reduce(jnp.maximum, tiles + near_pieces).max(axis=1, keepdims=True)
            mixed = None
            for n, part in enumerate(pieces + near_pieces):
                probs = jnp.exp2((part - peak) * FACTOR).astype(jnp.bfloat16)
                if n < len(pieces):
                    values = va[n * PIECE : (n + 1) * PIECE, :]
                else:
                    values = nva[pl.ds(starts[n - len(pieces)], ROWS), :]
                one = jnp.dot(probs, values, preferred_element_type=jnp.float32)
                mixed = one if mixed is None else mixed + one
            at = (h - heads_of[0] * GROUP) * HD
            out_ref[:, at : at + HD] = (mixed[:, :HD] / mixed[:, HD:]).astype(jnp.bfloat16)


def attention(ids, slash, q, prev, new, verts, back, heads_of=tuple(range(KVL))):
    keys, near = len(verts) * verts[0].shape[0] * BLK, 2 * prev.shape[1]
    scores = ROWS * len(heads_of) * GROUP * keys
    return pl.pallas_call(
        functools.partial(attention_kernel, back=back, heads_of=heads_of),
        out_shape=jax.ShapeDtypeStruct((ROWS, len(heads_of) * GROUP * HD), jnp.bfloat16),
        in_specs=[SM, SM] + [VM] * (3 + len(verts)),
        out_specs=VM,
        scratch_shapes=[
            pltpu.VMEM((keys, 2 * HD), jnp.bfloat16),
            pltpu.VMEM((near, HD), jnp.bfloat16),
            pltpu.VMEM((near, 2 * HD), jnp.bfloat16),
        ],
        compiler_params=pltpu.CompilerParams(vmem_limit_bytes=20 * 2**20),
        cost_estimate=pl.CostEstimate(
            flops=8 * scores * HD, bytes_accessed=2**22, transcendentals=scores
        ),
    )(ids, slash, q, prev, new, *verts)


def split_kernel(rows, out, sems):
    width = out.shape[2]
    copies = [
        pltpu.make_async_copy(rows.at[:, i * width : (i + 1) * width], out.at[i], sems.at[i])
        for i in range(SIDE)
    ]
    for copy in copies:
        copy.start()
    for copy in copies:
        copy.wait()


def join_kernel(ids, *refs, steps):
    ins, out, sems = refs[: len(steps)], refs[-2], refs[-1]
    width = KVL * GROUP * HD
    copies = []
    for n, (d, kv) in enumerate(steps):
        at = ((ids[3] + d) & (SIDE - 1)) * width + kv * GROUP * HD
        at = pl.multiple_of(at, GROUP * HD)
        copies.append(pltpu.make_async_copy(ins[n], out.at[:, pl.ds(at, ins[n].shape[1])], sems.at[n]))
    for copy in copies:
        copy.start()
    for copy in copies:
        copy.wait()


def join(ids, answers, steps, shape):
    return pl.pallas_call(
        functools.partial(join_kernel, steps=steps),
        out_shape=jax.ShapeDtypeStruct(shape, jnp.bfloat16),
        in_specs=[SM] + [VM] * len(steps),
        out_specs=ANY,
        scratch_shapes=[pltpu.SemaphoreType.DMA((len(steps),))],
        compiler_params=pltpu.CompilerParams(vmem_limit_bytes=8 * 2**20),
    )(ids, *[answers[step] for step in steps])


def local(queries, new_kv, cache_kv, vertical_blocks, slash_offsets):
    seq, z = lax.axis_index("seq"), lax.axis_index("kvh")
    ids = jnp.stack([seq // 8, seq // 2 % SIDE, seq % 2, z]).astype(jnp.int32)
    owner = vertical_blocks // CACHE_BLOCKS
    key = (owner % 2 * 16 + owner // 2 % SIDE * SIDE + owner // 8) * CACHE_BLOCKS
    key = key + vertical_blocks % CACHE_BLOCKS
    place = jnp.sum(key[:, None, :] < key[:, :, None], axis=2)
    entries = key.shape[1]
    order = jnp.sum(
        jnp.where(place[:, :, None] == jnp.arange(entries)[None, None, :], key[:, :, None], 0), axis=1
    )
    width = queries.shape[1] // SIDE
    asked = pl.pallas_call(
        split_kernel,
        out_shape=jax.ShapeDtypeStruct((SIDE, ROWS, width), jnp.bfloat16),
        in_specs=[ANY],
        out_specs=VM,
        scratch_shapes=[pltpu.SemaphoreType.DMA((SIDE,))],
        compiler_params=pltpu.CompilerParams(vmem_limit_bytes=60 * 2**20),
    )(queries)
    asked = lax.all_to_all(asked, "kvh", split_axis=0, concat_axis=0, tiled=True)

    tail = jnp.where(seq == 31, cache_kv[:, cache_kv.shape[1] - new_kv.shape[1] :, :], new_kv)
    prev = lax.ppermute(tail, "seq", [(i, (i + 1) % 32) for i in range(32)])

    picked = pl.pallas_call(
        pick_kernel,
        out_shape=[SLOT] * SIDE,
        in_specs=[SM, SM, ANY],
        out_specs=[VM] * SIDE,
        scratch_shapes=[pltpu.SemaphoreType.DMA((SIDE, KVL, 2))],
    )(ids, order, cache_kv)
    got = [picked[0]] + [along_x(picked[d], d) for d in range(1, SIDE)]
    to_y = pl.pallas_call(
        to_y_kernel,
        out_shape=[SLOT] * SIDE,
        in_specs=[SM, SM] + [VM] * SIDE,
        out_specs=[VM] * SIDE,
    )(ids, order, *got)
    got = [to_y[0]] + [along_y(to_y[d], d) for d in range(1, SIDE)]
    keep, send = pl.pallas_call(
        home_kernel,
        out_shape=[SLOT] * 2,
        in_specs=[SM, SM] + [VM] * SIDE,
        out_specs=[VM] * 2,
    )(ids, order, *got)
    swapped = other_core(send)
    at = SIDE * (ids[1] + SIDE * ids[2]) + ids[0]
    home = lax.dynamic_slice_in_dim(order, at, 1, axis=1) // (16 * CACHE_BLOCKS)
    home = jnp.where((home == ids[2])[:, :, None, None], keep, swapped)
    column = jnp.stack([home] + [along_y(home, d) for d in range(1, SIDE)])
    column, asked, prev, slash = lax.optimization_barrier((column, asked, prev, slash_offsets))
    plane = [column] + [along_x(column, d) for d in range(1, SIDE)]
    plane += [other_core(part) for part in plane]

    answers = {}
    for d, kvs in ((2, (0, 1)), (1, (0, 1)), (3, (0,)), (3, (1,)), (0, (0, 1))):
        done = attention(ids, slash, asked, prev, new_kv, plane, d, kvs)
        answers[d, kvs[0]] = along_z(done, SIDE - d) if d else done
    return join(ids, answers, ((0, 0), (1, 0), (2, 0), (3, 0), (3, 1)), queries.shape)


def solution(mesh):
    in_specs = (
        P(("seq", "kvh"), None),
        P(None, "seq", "kvh"),
        P(None, "seq", "kvh"),
        P("kvh", None),
        P("kvh", None),
    )
    out_specs = P(("seq", "kvh"), None)
    return jax.shard_map(local, mesh=mesh, in_specs=in_specs, out_specs=out_specs, check_vma=False)
```
